512 devices in a mesh: dp: 8 (over z_lo), row: 8 (over x, core), col: 8 (over z_hi, y).
Axes of the slice: x: 4, y: 4, z: 16 (z_hi: 2, z_lo: 8; z = z_hi * 8 + z_lo), core: 2. Of those that a mesh axis runs over, the one named last changes fastest.
Arguments:
- patches: bfloat16 [512, 6144], P(('dp', 'row'), 'col'), may hold values from -6 to 6
- w_up: bfloat16 [6144, 24576], P('col', ('dp', 'row')), may hold values from -0.078125 to 0.078125
- w_down: bfloat16 [24576, 6144], P(('dp', 'row'), 'col'), may hold values from -0.0390625 to 0.0390625
- owner_route: int32 [512], P(('dp', 'row')), may hold values from 0 to 7, as said below
- tok_grad: bfloat16 [512, 6144], P(('dp', 'row'), 'col'), may hold values from -0.1875 to 0.1875
- pool_grad: bfloat16 [64, 6144], P(('dp', 'row'), 'col'), may hold values from -1.5 to 1.5
Outputs:
- mixed: bfloat16 [512, 6144], P(('dp', 'row'), 'col')
- pooled: float32 [64, 6144], P(('dp', 'row'), 'col')
- grad_up: float32 [6144, 24576], P('col', ('dp', 'row'))
- grad_down: float32 [24576, 6144], P(('dp', 'row'), 'col')
The draws below stay inside these ranges and needn't reach their ends.
Inputs may be any that keep to these rules, and one draw needn't show every extreme that they name: `owner_route`: each device of dp and row holds 8 tokens, of which at most 2 name any one owner; in every dp group some owner is named exactly 2 times by every device of that group, and some other owner by no device of that group.
All inputs are finite; a program needn't handle non-finite values.
Results may differ from the reference program's by a relative error of at most 0.0054.
Values may be sent and summed in bfloat16 or wider, within the bound.
No kernel may reach another device: no remote copies, remote signals or barrier semaphores. Data moves between devices by JAX's collectives and lax.ppermute only.
A program may use at most 64 MiB of HBM per device.

```python
import math
import jax
import jax.numpy as jnp

D = 6144
FF = 24576
TOK_DEV = 8
CAP = 2
TOKENS = 512
NIMG = 64
N_DP = 8
N_ROW = 8


def draw_owner_route(key, part):
    key = jax.random.fold_in(key, 11)
    pool_len = N_ROW * CAP
    empty_shift = jax.random.randint(jax.random.fold_in(key, 1), (), 0, N_ROW).astype(jnp.int32)
    group_ids = jnp.arange(N_DP, dtype=jnp.int32)
    empty_owners = ((group_ids + empty_shift) % N_ROW).astype(jnp.int32)
    hot_steps = jax.random.randint(jax.random.fold_in(key, 2), (N_DP,), 1, N_ROW).astype(jnp.int32)
    hot_owners = ((empty_owners + hot_steps) % N_ROW).astype(jnp.int32)
    owners = (jnp.arange(pool_len, dtype=jnp.int32) // CAP).astype(jnp.int32)
    copy_index = (jnp.arange(pool_len, dtype=jnp.int32) % CAP).astype(jnp.int32)

    def one_device(device_index):
        device_key = jax.random.fold_in(key, device_index + 7)
        group_index = device_index // N_ROW
        own_index = device_index % N_ROW
        hot_owner = hot_owners[group_index]
        empty_owner = empty_owners[group_index]
        shuffle = jax.random.permutation(jax.random.fold_in(device_key, 1), pool_len).astype(jnp.int32)
        first_hot = owners == hot_owner
        first_own = (owners == own_index) & (copy_index == 0) & (own_index != hot_owner) & (own_index != empty_owner)
        never = owners == empty_owner
        scores = shuffle + jnp.where(first_hot, -2 * pool_len, 0) + jnp.where(first_own, -pool_len, 0) + jnp.where(never, 4 * pool_len, 0)
        chosen = owners[jnp.argsort(scores)][:TOK_DEV]
        row_order = jax.random.permutation(jax.random.fold_in(device_key, 2), TOK_DEV).astype(jnp.int32)
        return chosen[row_order]
    all_devices = jax.vmap(one_device)(jnp.arange(N_DP * N_ROW, dtype=jnp.int32))
    return all_devices.reshape(-1).astype(jnp.int32)


def shard_levels(rng, dims, split, smallest, high):
    level, own = 1.0, jax.random.fold_in(rng, 6)
    for position, shards_of in split:
        steps = jnp.exp(jax.random.uniform(jax.random.fold_in(own, position), (shards_of,), jnp.float32, smallest / len(split), high / len(split)))
        level = level * jnp.repeat(steps, dims[position] // shards_of).reshape([-1 if axis == position else 1 for axis in range(len(dims))])
    return level


def scatter_about(own_key, shape, spread, bound, pieces=(), kind=jnp.bfloat16):
    level = shard_levels(own_key, shape, pieces, -0.22, 0.18) if pieces else 1.0
    drawn = jax.random.normal(own_key, shape, jnp.float32) * spread * level
    return jnp.minimum(jnp.maximum(drawn, -bound), bound).astype(kind)


def setup_inputs(seed: int = 0) -> dict:
    key_list = jax.random.split(jax.random.key(seed), 7)
    return {
        "patches": scatter_about(key_list[0], (TOKENS, D), 1.0, 6.0, ((0, 64), (1, 8))),
        "w_up": scatter_about(key_list[1], (D, FF), D ** -0.5, 0.078125, ((0, 8), (1, 64))),
        "w_down": scatter_about(key_list[2], (FF, D), FF ** -0.5, 0.0390625, ((0, 64), (1, 8))),
        "owner_route": draw_owner_route(jax.random.fold_in(key_list[6], 71), 0),
        "tok_grad": scatter_about(key_list[4], (TOKENS, D), 0.03, 0.1875, ((0, 64), (1, 8))),
        "pool_grad": scatter_about(key_list[5], (NIMG, D), 0.25, 1.5, ((0, 64), (1, 8))),
    }


GELU_SCALE = math.sqrt(2.0 / math.pi)

def gelu_tanh(inner):
    return 0.5 * inner * (1.0 + jnp.tanh(GELU_SCALE * (inner + 0.044715 * inner * inner * inner)))

def gelu_slope(inner):
    tanh_term = jnp.tanh(GELU_SCALE * (inner + 0.044715 * inner * inner * inner))
    return 0.5 * (1.0 + tanh_term) + 0.5 * inner * (1.0 - tanh_term * tanh_term) * GELU_SCALE * (1.0 + 3.0 * 0.044715 * inner * inner)

def reference(patches, w_up, w_down, owner_route, tok_grad, pool_grad):
    preact = jnp.dot(patches, w_up, preferred_element_type=jnp.float32)
    hidden = gelu_tanh(preact).astype(jnp.bfloat16)
    mixed = jnp.dot(hidden, w_down, preferred_element_type=jnp.float32).astype(jnp.bfloat16)
    token_pos = jnp.arange(TOKENS, dtype=jnp.int32)
    image_index = (N_ROW * (token_pos // (N_ROW * TOK_DEV)) + owner_route).astype(jnp.int32)
    image_count = jax.ops.segment_sum(jnp.ones((TOKENS,), jnp.float32), image_index, num_segments=NIMG)
    image_total = jax.ops.segment_sum(mixed.astype(jnp.float32), image_index, num_segments=NIMG)
    divisor = jnp.maximum(image_count, 1.0)
    pooled = image_total / divisor[:, None]
    image_grad = (pool_grad.astype(jnp.float32) / divisor[:, None]).astype(jnp.bfloat16)
    grad_mixed = (tok_grad.astype(jnp.float32) + image_grad[image_index].astype(jnp.float32)).astype(jnp.bfloat16)
    grad_hidden = jnp.dot(grad_mixed, w_down.T, preferred_element_type=jnp.float32)
    grad_preact = (grad_hidden * gelu_slope(preact)).astype(jnp.bfloat16)
    grad_down = jnp.dot(hidden.T, grad_mixed, preferred_element_type=jnp.float32)
    grad_up = jnp.dot(patches.T, grad_preact, preferred_element_type=jnp.float32)
    return (mixed, pooled, grad_up, grad_down)
```

```python
import math

import jax
import jax.numpy as jnp
from jax import lax
from jax.sharding import PartitionSpec as P

GELU_SCALE = math.sqrt(2.0 / math.pi)
BF = jnp.bfloat16
F32 = jnp.float32
LANES = 128

Y_GROUPS = [[0, 1, 2, 3], [4, 5, 6, 7]]
X_GROUPS = [[0, 2, 4, 6], [1, 3, 5, 7]]
CORE_GROUPS = [[0, 1], [2, 3], [4, 5], [6, 7]]
Z_SWAP = [(i, (i + 4) % 8) for i in range(8)]


def spread(block, axis, count, groups=None):
    copies = jnp.broadcast_to(block[None], (count,) + block.shape)
    return lax.all_to_all(copies, axis, split_axis=0, concat_axis=0, tiled=True, axis_index_groups=groups)


def exchange(blocks, axis, groups=None):
    return lax.all_to_all(blocks, axis, split_axis=0, concat_axis=0, tiled=True, axis_index_groups=groups)


def local(patches, w_up, w_down, owner_route, tok_grad, pool_grad):
    tok, width = patches.shape
    hid = w_up.shape[1]
    pieces = width // LANES

    side = jnp.concatenate(
        [
            pool_grad.reshape(pieces, LANES),
            jnp.pad(owner_route.astype(BF)[None, :], ((0, 0), (0, LANES - tok))),
            jnp.zeros((tok - pieces - 1, LANES), BF),
        ],
        axis=0,
    )
    block = jnp.concatenate([patches, tok_grad, side], axis=1)
    got = spread(block, "dp", 8)
    got = got.reshape(64, 2 * width + LANES)
    got = spread(got, "row", 4, X_GROUPS)
    got = got.reshape(256, 2 * width + LANES)
    got = spread(got, "row", 2, CORE_GROUPS)
    got = got.reshape(512, 2 * width + LANES)

    rows = got[:, :width]
    tgrads = got[:, width : 2 * width]
    sides = got[:, 2 * width :].reshape(64, tok, LANES)
    pools = sides[:, :pieces, :].reshape(64, width)
    route = sides[:, pieces, :tok].astype(jnp.int32)
    dp_of = lax.broadcasted_iota(jnp.int32, (64, tok), 0) % 8
    image = ((route % 2) * 4 + route // 2) * 8 + dp_of
    image = image.reshape(512, 1)
    onehot = (image == lax.broadcasted_iota(jnp.int32, (512, 64), 1)).astype(BF)
    count = jnp.maximum(jnp.sum(onehot.astype(F32), axis=0), 1.0)[:, None]
    image_grad = (pools.astype(F32) / count).astype(BF)
    returned = jnp.dot(onehot, image_grad, preferred_element_type=F32)
    grads = (tgrads.astype(F32) + returned).astype(BF)

    up = jnp.dot(rows, w_up, preferred_element_type=F32)
    back = lax.dot_general(grads, w_down, (((1,), (1,)), ((), ())), preferred_element_type=F32)
    both = jnp.concatenate([up.astype(BF), back.astype(BF)], axis=1).reshape(4, 128, 2 * hid)
    part = exchange(both, "col", Y_GROUPS)
    part = jnp.sum(part.astype(F32), axis=0).astype(BF)
    other = lax.ppermute(part, "col", Z_SWAP)
    total = part.astype(F32) + other.astype(F32)
    v = total[:, :hid]
    s = jnp.tanh(GELU_SCALE * (v + 0.044715 * v * v * v))
    hidden = (0.5 * v * (1.0 + s)).astype(BF)
    slope = 0.5 * (1.0 + s) + 0.5 * v * (1.0 - s * s) * GELU_SCALE * (1.0 + 3.0 * 0.044715 * v * v)
    gp = (total[:, hid:] * slope).astype(BF)
    hg = spread(jnp.concatenate([hidden, gp], axis=1), "col", 4, Y_GROUPS).reshape(512, 2 * hid)
    hidden = hg[:, :hid]
    gp = hg[:, hid:]

    down = jnp.dot(hidden, w_down, preferred_element_type=F32)
    pooled_part = (
        lax.dot_general(onehot, down.astype(BF), (((0,), (0,)), ((), ())), preferred_element_type=F32) / count
    )
    packed = jnp.pad(pooled_part.astype(BF).reshape(64, pieces, LANES), ((0, 0), (0, tok - pieces), (0, 0)))
    down = jnp.concatenate([down.astype(BF), packed.reshape(512, LANES)], axis=1)
    down = down.reshape(2, 4, 64, width + LANES).transpose(1, 0, 2, 3).reshape(8, 64, width + LANES)
    half = exchange(down, "row")
    half = jnp.sum(half.astype(F32), axis=0).astype(BF).reshape(8, tok, width + LANES)
    last = exchange(half, "dp")
    last = jnp.sum(last.astype(F32), axis=0)
    mixed = last[:, :width].astype(BF)
    pooled = last[:pieces, width:].reshape(1, width)

    grad_down = lax.dot_general(hidden, grads, (((0,), (0,)), ((), ())), preferred_element_type=F32)
    grad_up = lax.dot_general(rows, gp, (((0,), (0,)), ((), ())), preferred_element_type=F32)
    return (mixed, pooled, grad_up, grad_down)


def solution(mesh):
    in_specs = (
        P(("dp", "row"), "col"),
        P("col", ("dp", "row")),
        P(("dp", "row"), "col"),
        P(("dp", "row")),
        P(("dp", "row"), "col"),
        P(("dp", "row"), "col"),
    )
    out_specs = (
        P(("dp", "row"), "col"),
        P(("dp", "row"), "col"),
        P("col", ("dp", "row")),
        P(("dp", "row"), "col"),
    )
    return jax.shard_map(local, mesh=mesh, in_specs=in_specs, out_specs=out_specs, check_vma=False)
```

```python
import math

import jax
import jax.numpy as jnp
from jax import lax
from jax.sharding import PartitionSpec as P

GELU_SCALE = math.sqrt(2.0 / math.pi)
BF = jnp.bfloat16
F16 = jnp.float16
F32 = jnp.float32
LANES = 128
UP_SCALE = 32.0

Y_GROUPS = [[0, 1, 2, 3], [4, 5, 6, 7]]
X_GROUPS = [[0, 2, 4, 6], [1, 3, 5, 7]]
CORE_GROUPS = [[0, 1], [2, 3], [4, 5], [6, 7]]
Z_SWAP = [(i, (i + 4) % 8) for i in range(8)]
CORE_SWAP = [(i, i ^ 1) for i in range(8)]


def spread(block, axis, count, groups=None):
    copies = jnp.broadcast_to(block[None], (count,) + block.shape)
    return lax.all_to_all(copies, axis, split_axis=0, concat_axis=0, tiled=True, axis_index_groups=groups)


def exchange(blocks, axis, groups=None):
    return lax.all_to_all(blocks, axis, split_axis=0, concat_axis=0, tiled=True, axis_index_groups=groups)


def local(patches, w_up, w_down, owner_route, tok_grad, pool_grad):
    tok, width = patches.shape
    hid = w_up.shape[1]
    pieces = width // LANES

    side = jnp.concatenate(
        [
            pool_grad.reshape(pieces, LANES),
            jnp.pad(owner_route.astype(BF)[None, :], ((0, 0), (0, LANES - tok))),
            jnp.zeros((tok - pieces - 1, LANES), BF),
        ],
        axis=0,
    )
    block = jnp.concatenate([patches, tok_grad, side], axis=1)
    got = spread(block, "dp", 8)
    got = got.reshape(64, 2 * width + LANES)
    got = spread(got, "row", 4, X_GROUPS)
    got = got.reshape(256, 2 * width + LANES)
    rows = spread(got[:, :width], "row", 2, CORE_GROUPS).reshape(512, width)

    up = jnp.dot(rows, w_up, preferred_element_type=F32) * UP_SCALE
    up = exchange(up.astype(F16).reshape(4, 128, hid), "col", Y_GROUPS)
    up = jnp.sum(up.astype(F32), axis=0).astype(F16)
    other = lax.ppermute(up, "col", Z_SWAP)

    own_g = got[:, width:]
    sib_g = lax.ppermute(own_g, "row", CORE_SWAP)
    first = lax.axis_index("row") % 2 == 0
    got_g = jnp.concatenate([jnp.where(first, own_g, sib_g), jnp.where(first, sib_g, own_g)], axis=0)
    tgrads = got_g[:, :width]
    sides = got_g[:, width:].reshape(64, tok, LANES)
    pools = sides[:, :pieces, :].reshape(64, width)
    route = sides[:, pieces, :tok].astype(jnp.int32)
    dp_of = lax.broadcasted_iota(jnp.int32, (64, tok), 0) % 8
    image = ((route % 2) * 4 + route // 2) * 8 + dp_of
    image = image.reshape(512, 1)
    onehot = (image == lax.broadcasted_iota(jnp.int32, (512, 64), 1)).astype(BF)
    count = jnp.maximum(jnp.sum(onehot.astype(F32), axis=0), 1.0)[:, None]
    image_grad = (pools.astype(F32) / count).astype(BF)
    returned = jnp.dot(onehot, image_grad, preferred_element_type=F32)
    grads = (tgrads.astype(F32) + returned).astype(BF)
    back = lax.dot_general(grads, w_down, (((1,), (1,)), ((), ())), preferred_element_type=F32)

    v = (up.astype(F32) + other.astype(F32)) * (1.0 / UP_SCALE)
    s = jnp.tanh(GELU_SCALE * (v + 0.044715 * v * v * v))
    hidden = (0.5 * v * (1.0 + s)).astype(BF)
    slope = 0.5 * (1.0 + s) + 0.5 * v * (1.0 - s * s) * GELU_SCALE * (1.0 + 3.0 * 0.044715 * v * v)

    mix = jnp.concatenate(
        [jnp.broadcast_to(hidden[None], (4, 128, hid)), back.astype(BF).reshape(4, 128, hid)], axis=2
    )
    mix = exchange(mix, "col", Y_GROUPS)
    hidden = mix[:, :, :hid].reshape(512, hid)
    back = jnp.sum(mix[:, :, hid:].astype(F32), axis=0)

    down = jnp.dot(hidden, w_down, preferred_element_type=F32)
    pooled_part = (
        lax.dot_general(onehot, down.astype(BF), (((0,), (0,)), ((), ())), preferred_element_type=F32) / count
    )
    packed = jnp.pad(pooled_part.astype(BF).reshape(64, pieces, LANES), ((0, 0), (0, tok - pieces), (0, 0)))
    down = jnp.concatenate([down.astype(BF), packed.reshape(512, LANES)], axis=1)
    down = down.reshape(2, 4, 64, width + LANES).transpose(1, 0, 2, 3).reshape(8, 64, width + LANES)
    half = exchange(down, "row")
    half = jnp.sum(half.astype(F32), axis=0).astype(BF).reshape(8, tok, width + LANES)

    back_other = lax.ppermute(back.astype(BF), "col", Z_SWAP)
    gp = ((back + back_other.astype(F32)) * slope).astype(BF)
    grad_down = lax.dot_general(hidden, grads, (((0,), (0,)), ((), ())), preferred_element_type=F32)
    half, grad_down = lax.optimization_barrier((half, grad_down))
    last = exchange(half, "dp")
    last = jnp.sum(last.astype(F32), axis=0)
    mixed = last[:, :width].astype(BF)
    pooled = last[:pieces, width:].reshape(1, width)

    y = lax.axis_index("col") % 4
    gps = [gp] + [
        lax.ppermute(gp, "col", [(i, i // 4 * 4 + (i - k) % 4) for i in range(8)]) for k in (1, 2, 3)
    ]
    turned = lax.dynamic_slice(jnp.concatenate([rows, rows], axis=0), (y * 128, 0), (512, width))
    grad_up = lax.dot_general(
        turned, jnp.concatenate(gps, axis=0), (((0,), (0,)), ((), ())), preferred_element_type=F32
    )
    return (mixed, pooled, grad_up, grad_down)


def solution(mesh):
    in_specs = (
        P(("dp", "row"), "col"),
        P("col", ("dp", "row")),
        P(("dp", "row"), "col"),
        P(("dp", "row")),
        P(("dp", "row"), "col"),
        P(("dp", "row"), "col"),
    )
    out_specs = (
        P(("dp", "row"), "col"),
        P(("dp", "row"), "col"),
        P("col", ("dp", "row")),
        P(("dp", "row"), "col"),
    )
    return jax.shard_map(local, mesh=mesh, in_specs=in_specs, out_specs=out_specs, check_vma=False)
```

```python
import math

import jax
import jax.numpy as jnp
from jax import lax
from jax.sharding import PartitionSpec as P

GELU_SCALE = math.sqrt(2.0 / math.pi)
BF = jnp.bfloat16
F16 = jnp.float16
F32 = jnp.float32
LANES = 128
UP_SCALE = 32.0

Y_GROUPS = [[0, 1, 2, 3], [4, 5, 6, 7]]
X_GROUPS = [[0, 2, 4, 6], [1, 3, 5, 7]]
CORE_GROUPS = [[0, 1], [2, 3], [4, 5], [6, 7]]
Z_SWAP = [(i, (i + 4) % 8) for i in range(8)]
CORE_SWAP = [(i, i ^ 1) for i in range(8)]


def spread(block, axis, count, groups=None):
    copies = jnp.broadcast_to(block[None], (count,) + block.shape)
    return lax.all_to_all(copies, axis, split_axis=0, concat_axis=0, tiled=True, axis_index_groups=groups)


def gather(block, axis, groups):
    return lax.all_gather(block, axis, axis=0, tiled=True, axis_index_groups=groups)


def exchange(blocks, axis, groups=None):
    return lax.all_to_all(blocks, axis, split_axis=0, concat_axis=0, tiled=True, axis_index_groups=groups)


def local(patches, w_up, w_down, owner_route, tok_grad, pool_grad):
    tok, width = patches.shape
    hid = w_up.shape[1]
    pieces = width // LANES

    side = jnp.concatenate(
        [
            pool_grad.reshape(pieces, LANES),
            jnp.pad(owner_route.astype(BF)[None, :], ((0, 0), (0, LANES - tok))),
            jnp.zeros((tok - pieces - 1, LANES), BF),
        ],
        axis=0,
    )
    block = jnp.concatenate([patches, tok_grad, side], axis=1)
    got = spread(block, "dp", 8)
    got = got.reshape(64, 2 * width + LANES)
    got = gather(got, "row", X_GROUPS)
    rows = gather(got[:, :width], "row", CORE_GROUPS)

    up = jnp.dot(rows, w_up, preferred_element_type=F32) * UP_SCALE
    up = up.astype(F16)
    up = exchange(up.reshape(4, 128, hid), "col", Y_GROUPS)
    up = jnp.sum(up.astype(F32), axis=0).astype(F16)
    other = lax.ppermute(up, "col", Z_SWAP)
    own_g, _ = lax.optimization_barrier((got[:, width:], up))

    got_g = gather(own_g, "row", CORE_GROUPS)
    tgrads = got_g[:, :width]
    sides = got_g[:, width:].reshape(64, tok, LANES)
    pools = sides[:, :pieces, :].reshape(64, width)
    route = sides[:, pieces, :tok].astype(jnp.int32)
    dp_of = lax.broadcasted_iota(jnp.int32, (64, tok), 0) % 8
    image = ((route % 2) * 4 + route // 2) * 8 + dp_of
    image = image.reshape(512, 1)
    onehot = (image == lax.broadcasted_iota(jnp.int32, (512, 64), 1)).astype(BF)
    count = jnp.maximum(jnp.sum(onehot.astype(F32), axis=0), 1.0)[:, None]
    image_grad = (pools.astype(F32) / count).astype(BF)
    returned = jnp.dot(onehot, image_grad, preferred_element_type=F32)
    grads = (tgrads.astype(F32) + returned).astype(BF)
    back = lax.dot_general(grads, w_down, (((1,), (1,)), ((), ())), preferred_element_type=F32)

    v = (up.astype(F32) + other.astype(F32)) * (1.0 / UP_SCALE)
    s = jnp.tanh(GELU_SCALE * (v + 0.044715 * v * v * v))
    hidden = (0.5 * v * (1.0 + s)).astype(BF)
    slope = 0.5 * (1.0 + s) + 0.5 * v * (1.0 - s * s) * GELU_SCALE * (1.0 + 3.0 * 0.044715 * v * v)

    mix = jnp.concatenate(
        [jnp.broadcast_to(hidden[None], (4, 128, hid)), back.astype(BF).reshape(4, 128, hid)], axis=2
    )
    mix = exchange(mix, "col", Y_GROUPS)
    hidden = mix[:, :, :hid].reshape(512, hid)
    back = jnp.sum(mix[:, :, hid:].astype(F32), axis=0)

    down = jnp.dot(hidden, w_down, preferred_element_type=F32)
    pooled_part = (
        lax.dot_general(onehot, down.astype(BF), (((0,), (0,)), ((), ())), preferred_element_type=F32) / count
    )
    packed = jnp.pad(pooled_part.astype(BF).reshape(64, pieces, LANES), ((0, 0), (0, tok - pieces), (0, 0)))
    down = jnp.concatenate([down.astype(BF), packed.reshape(512, LANES)], axis=1)
    down = down.reshape(2, 256, width + LANES)
    core = lax.axis_index("row") % 2
    sent = lax.dynamic_index_in_dim(down, 1 - core, 0, keepdims=False)
    sent = gather(sent, "row", CORE_GROUPS).reshape(2, 256, width + LANES)
    half = lax.dynamic_index_in_dim(down, core, 0).astype(F32)
    half = half + lax.dynamic_index_in_dim(sent, 1 - core, 0).astype(F32)
    half = half.astype(BF).reshape(4, 64, width + LANES)
    back, _ = lax.optimization_barrier((back, half))
    half = exchange(half, "row", X_GROUPS)
    half = jnp.sum(half.astype(F32), axis=0).astype(BF).reshape(8, tok, width + LANES)

    back_other = lax.ppermute(back.astype(BF), "col", Z_SWAP)
    gp = ((back + back_other.astype(F32)) * slope).astype(BF)
    grad_down = lax.dot_general(hidden, grads, (((0,), (0,)), ((), ())), preferred_element_type=F32)
    half, grad_down = lax.optimization_barrier((half, grad_down))
    last = exchange(half, "dp")
    last = jnp.sum(last.astype(F32), axis=0)
    mixed = last[:, :width].astype(BF)
    pooled = last[:pieces, width:].reshape(1, width)

    y = lax.axis_index("col") % 4
    gps = [gp] + [
        lax.ppermute(gp, "col", [(i, i // 4 * 4 + (i - k) % 4) for i in range(8)]) for k in (1, 2, 3)
    ]
    turned = lax.dynamic_slice(jnp.concatenate([rows, rows], axis=0), (y * 128, 0), (512, width))
    grad_up = lax.dot_general(
        turned, jnp.concatenate(gps, axis=0), (((0,), (0,)), ((), ())), preferred_element_type=F32
    )
    return (mixed, pooled, grad_up, grad_down)


def solution(mesh):
    in_specs = (
        P(("dp", "row"), "col"),
        P("col", ("dp", "row")),
        P(("dp", "row"), "col"),
        P(("dp", "row")),
        P(("dp", "row"), "col"),
        P(("dp", "row"), "col"),
    )
    out_specs = (
        P(("dp", "row"), "col"),
        P(("dp", "row"), "col"),
        P("col", ("dp", "row")),
        P(("dp", "row"), "col"),
    )
    return jax.shard_map(local, mesh=mesh, in_specs=in_specs, out_specs=out_specs, check_vma=False)
```

```python
import math

import jax
import jax.numpy as jnp
from jax import lax
from jax.experimental import pallas as pl
from jax.experimental.pallas import tpu as pltpu
from jax.sharding import PartitionSpec as P

GELU_SCALE = math.sqrt(2.0 / math.pi)
BF = jnp.bfloat16
F16 = jnp.float16
F32 = jnp.float32
LANES = 128
UP_SCALE = 32.0

Y_GROUPS = [[0, 1, 2, 3], [4, 5, 6, 7]]
X_GROUPS = [[0, 2, 4, 6], [1, 3, 5, 7]]
CORE_GROUPS = [[0, 1], [2, 3], [4, 5], [6, 7]]
Z_SWAP = [(i, (i + 4) % 8) for i in range(8)]
CORE_SWAP = [(i, i ^ 1) for i in range(8)]


def spread(block, axis, count, groups=None):
    copies = jnp.broadcast_to(block[None], (count,) + block.shape)
    return lax.all_to_all(copies, axis, split_axis=0, concat_axis=0, tiled=True, axis_index_groups=groups)


def gather(block, axis, groups):
    return lax.all_gather(block, axis, axis=0, tiled=True, axis_index_groups=groups)


def exchange(blocks, axis, groups=None):
    return lax.all_to_all(blocks, axis, split_axis=0, concat_axis=0, tiled=True, axis_index_groups=groups)


def pack_kernel(route_ref, patches_ref, tgrad_ref, pool_ref, out_ref):
    width = patches_ref.shape[1]
    pieces = width // LANES
    tok = patches_ref.shape[0]
    lane = lax.broadcasted_iota(jnp.int32, (tok, LANES), 1)
    sub = lax.broadcasted_iota(jnp.int32, (tok, LANES), 0)
    side = jnp.zeros((tok, LANES), F32)
    for j in range(pieces):
        piece = pool_ref[:, j * LANES : (j + 1) * LANES].astype(F32)
        side = jnp.where(sub == j, jnp.broadcast_to(piece, (tok, LANES)), side)
    for t in range(tok):
        side = jnp.where((sub == pieces) & (lane == t), route_ref[t].astype(F32), side)
    side = side.astype(BF)
    for k in range(out_ref.shape[0]):
        out_ref[k, :, :width] = patches_ref[...]
        out_ref[k, :, width : 2 * width] = tgrad_ref[...]
        out_ref[k, :, 2 * width :] = side


def grads_kernel(got_ref, w_ref, grads_ref, onehot_ref, count_ref, back_ref):
    tokens = got_ref.shape[0]
    width = w_ref.shape[1]
    side = got_ref[:, width:]
    sub = lax.broadcasted_iota(jnp.int32, (tokens, LANES), 0) % 8
    lane = lax.broadcasted_iota(jnp.int32, (tokens, LANES), 1)
    group = (
        lax.broadcasted_iota(jnp.int32, (tokens, 64), 0) // 8 == lax.broadcasted_iota(jnp.int32, (tokens, 64), 1)
    )
    group = group.astype(F32).astype(BF)
    down_rows = (((0,), (0,)), ((), ()))
    wide = jnp.where(sub == width // LANES, side.astype(F32), 0.0).astype(BF)
    routes = lax.dot_general(group, wide, down_rows, preferred_element_type=F32).astype(BF)
    routes = jnp.dot(group, routes, preferred_element_type=F32)
    route = jnp.sum(jnp.where(lane == sub, routes, 0.0), axis=1, keepdims=True).astype(jnp.int32)
    dp_of = (lax.broadcasted_iota(jnp.int32, (tokens, 1), 0) // 8) % 8
    image = ((route % 2) * 4 + route // 2) * 8 + dp_of
    onehot = (image == lax.broadcasted_iota(jnp.int32, (tokens, 64), 1)).astype(F32).astype(BF)
    ones = jnp.ones((tokens, LANES), BF)
    count = jnp.maximum(lax.dot_general(onehot, ones, down_rows, preferred_element_type=F32)[:, :1], 1.0)
    onehot_ref[...] = onehot
    count_ref[...] = count
    for j in range(width // LANES):
        piece = jnp.where(sub == j, side.astype(F32), 0.0).astype(BF)
        pool = lax.dot_general(group, piece, down_rows, preferred_element_type=F32)
        image_grad = (pool / count).astype(BF)
        returned = jnp.dot(onehot, image_grad, preferred_element_type=F32)
        cols = slice(j * LANES, (j + 1) * LANES)
        grads_ref[:, cols] = (got_ref[:, cols].astype(F32) + returned).astype(BF)
    back_ref[...] = lax.dot_general(
        grads_ref[...], w_ref[...], (((1,), (1,)), ((), ())), preferred_element_type=F32
    ).astype(BF)


def down_kernel(core_ref, mix_ref, w_ref, onehot_ref, count_ref, own_ref, sent_ref, back_ref, back_bf_ref):
    hid, width = w_ref.shape
    core = core_ref[0]
    back = mix_ref[0, :, hid:].astype(F32)
    for k in range(1, mix_ref.shape[0]):
        back = back + mix_ref[k, :, hid:].astype(F32)
    back_ref[...] = back
    back_bf_ref[...] = back.astype(BF)
    parts = []
    total = None
    for which in (core, 1 - core):
        rows = mix_ref[pl.ds(2 * which, 2), :, :hid].reshape(256, hid)
        part = jnp.dot(rows, w_ref[...], preferred_element_type=F32).astype(BF)
        marks = onehot_ref[pl.ds(pl.multiple_of(which * 256, 256), 256), :]
        image = lax.dot_general(marks, part, (((0,), (0,)), ((), ())), preferred_element_type=F32)
        total = image if total is None else total + image
        parts.append(part)
    mean = (total / count_ref[...]).astype(BF)
    row = lax.broadcasted_iota(jnp.int32, (256, 64), 0)
    image_of = lax.broadcasted_iota(jnp.int32, (256, 64), 1)
    sub = lax.broadcasted_iota(jnp.int32, (256, LANES), 0) % 8
    for which, part, ref in ((core, parts[0], own_ref), (1 - core, parts[1], sent_ref)):
        pick = ((row // 8 + which * 32) == image_of).astype(F32).astype(BF)
        wide = jnp.dot(pick, mean, preferred_element_type=F32)
        packed = jnp.zeros((256, LANES), F32)
        for j in range(width // LANES):
            packed = jnp.where(sub == j, wide[:, j * LANES : (j + 1) * LANES], packed)
        ref[:, :width] = part
        ref[:, width:] = packed.astype(BF)


def local(patches, w_up, w_down, owner_route, tok_grad, pool_grad):
    tok, width = patches.shape
    hid = w_up.shape[1]
    pieces = width // LANES

    got = pl.pallas_call(
        pack_kernel,
        out_shape=jax.ShapeDtypeStruct((8, tok, 2 * width + LANES), BF),
        in_specs=[pl.BlockSpec(memory_space=pltpu.SMEM)] + [pl.BlockSpec(memory_space=pltpu.VMEM)] * 3,
        cost_estimate=pl.CostEstimate(flops=100_000, bytes_accessed=300_000, transcendentals=0),
    )(owner_route, patches, tok_grad, pool_grad)
    got = exchange(got, "dp")
    got = got.reshape(64, 2 * width + LANES)
    got = gather(got, "row", X_GROUPS)
    rows = gather(got[:, :width], "row", CORE_GROUPS)

    up = jnp.dot(rows, w_up, preferred_element_type=F32) * UP_SCALE
    up = up.astype(F16)
    up = exchange(up.reshape(4, 128, hid), "col", Y_GROUPS)
    up = jnp.sum(up.astype(F32), axis=0).astype(F16)
    other = lax.ppermute(up, "col", Z_SWAP)
    own_g, _ = lax.optimization_barrier((got[:, width:], up))

    got_g = gather(own_g, "row", CORE_GROUPS)
    grads, onehot, count, back = pl.pallas_call(
        grads_kernel,
        out_shape=[
            jax.ShapeDtypeStruct((512, width), BF),
            jax.ShapeDtypeStruct((512, 64), BF),
            jax.ShapeDtypeStruct((64, 1), F32),
            jax.ShapeDtypeStruct((512, hid), BF),
        ],
        in_specs=[pl.BlockSpec(memory_space=pltpu.VMEM)] * 2,
        compiler_params=pltpu.CompilerParams(vmem_limit_bytes=24 * 1024 * 1024),
        cost_estimate=pl.CostEstimate(flops=1_000_000, bytes_accessed=100_000, transcendentals=0),
    )(got_g, w_down)

    v = (up.astype(F32) + other.astype(F32)) * (1.0 / UP_SCALE)
    s = jnp.tanh(GELU_SCALE * (v + 0.044715 * v * v * v))
    hidden = (0.5 * v * (1.0 + s)).astype(BF)
    slope = 0.5 * (1.0 + s) + 0.5 * v * (1.0 - s * s) * GELU_SCALE * (1.0 + 3.0 * 0.044715 * v * v)

    mix = jnp.concatenate(
        [jnp.broadcast_to(hidden[None], (4, 128, hid)), back.reshape(4, 128, hid)], axis=2
    )
    mix = exchange(mix, "col", Y_GROUPS)
    hidden = mix[:, :, :hid].reshape(512, hid)
    core = lax.axis_index("row") % 2
    wide = width + LANES
    own, sent, back, back_bf = pl.pallas_call(
        down_kernel,
        out_shape=[jax.ShapeDtypeStruct((256, wide), BF)] * 2
        + [jax.ShapeDtypeStruct((128, hid), F32), jax.ShapeDtypeStruct((128, hid), BF)],
        in_specs=[pl.BlockSpec(memory_space=pltpu.SMEM)] + [pl.BlockSpec(memory_space=pltpu.VMEM)] * 4,
        compiler_params=pltpu.CompilerParams(vmem_limit_bytes=24 * 1024 * 1024),
        cost_estimate=pl.CostEstimate(flops=400_000_000, bytes_accessed=3_000_000, transcendentals=0),
    )(core.astype(jnp.int32).reshape(1), mix, w_down, onehot, count)
    sent = gather(sent, "row", CORE_GROUPS).reshape(2, 256, wide)
    half = own.astype(F32) + lax.dynamic_index_in_dim(sent, 1 - core, 0, keepdims=False).astype(F32)
    half = half.astype(BF).reshape(4, 64, wide)
    back_bf, _ = lax.optimization_barrier((back_bf, half))
    half = exchange(half, "row", X_GROUPS)
    half = jnp.sum(half.astype(F32), axis=0).astype(BF).reshape(8, tok, width + LANES)

    back_other = lax.ppermute(back_bf, "col", Z_SWAP)
    gp = ((back + back_other.astype(F32)) * slope).astype(BF)
    grad_down = lax.dot_general(hidden, grads, (((0,), (0,)), ((), ())), preferred_element_type=F32)
    half, grad_down = lax.optimization_barrier((half, grad_down))
    last = exchange(half, "dp")
    last = jnp.sum(last.astype(F32), axis=0)
    mixed = last[:, :width].astype(BF)
    pooled = last[:pieces, width:].reshape(1, width)

    y = lax.axis_index("col") % 4
    gps = [gp] + [
        lax.ppermute(gp, "col", [(i, i // 4 * 4 + (i - k) % 4) for i in range(8)]) for k in (1, 2, 3)
    ]
    turned = lax.dynamic_slice(jnp.concatenate([rows, rows], axis=0), (y * 128, 0), (512, width))
    grad_up = lax.dot_general(
        turned, jnp.concatenate(gps, axis=0), (((0,), (0,)), ((), ())), preferred_element_type=F32
    )
    return (mixed, pooled, grad_up, grad_down)


def solution(mesh):
    in_specs = (
        P(("dp", "row"), "col"),
        P("col", ("dp", "row")),
        P(("dp", "row"), "col"),
        P(("dp", "row")),
        P(("dp", "row"), "col"),
        P(("dp", "row"), "col"),
    )
    out_specs = (
        P(("dp", "row"), "col"),
        P(("dp", "row"), "col"),
        P("col", ("dp", "row")),
        P(("dp", "row"), "col"),
    )
    return jax.shard_map(local, mesh=mesh, in_specs=in_specs, out_specs=out_specs, check_vma=False)
```

```python
import math

import jax
import jax.numpy as jnp
from jax import lax
from jax.experimental import pallas as pl
from jax.experimental.pallas import tpu as pltpu
from jax.sharding import PartitionSpec as P

GELU_SCALE = math.sqrt(2.0 / math.pi)
BF = jnp.bfloat16
F16 = jnp.float16
F32 = jnp.float32
LANES = 128
UP_SCALE = 32.0

Y_GROUPS = [[0, 1, 2, 3], [4, 5, 6, 7]]
X_GROUPS = [[0, 2, 4, 6], [1, 3, 5, 7]]
CORE_GROUPS = [[0, 1], [2, 3], [4, 5], [6, 7]]
Z_SWAP = [(i, (i + 4) % 8) for i in range(8)]
CORE_SWAP = [(i, i ^ 1) for i in range(8)]


def spread(block, axis, count, groups=None):
    copies = jnp.broadcast_to(block[None], (count,) + block.shape)
    return lax.all_to_all(copies, axis, split_axis=0, concat_axis=0, tiled=True, axis_index_groups=groups)


def gather(block, axis, groups):
    return lax.all_gather(block, axis, axis=0, tiled=True, axis_index_groups=groups)


def exchange(blocks, axis, groups=None):
    return lax.all_to_all(blocks, axis, split_axis=0, concat_axis=0, tiled=True, axis_index_groups=groups)


def pack_kernel(route_ref, patches_ref, tgrad_ref, pool_ref, out_ref):
    width = patches_ref.shape[1]
    pieces = width // LANES
    tok = patches_ref.shape[0]
    lane = lax.broadcasted_iota(jnp.int32, (tok, LANES), 1)
    sub = lax.broadcasted_iota(jnp.int32, (tok, LANES), 0)
    side = jnp.zeros((tok, LANES), F32)
    for j in range(pieces):
        piece = pool_ref[:, j * LANES : (j + 1) * LANES].astype(F32)
        side = jnp.where(sub == j, jnp.broadcast_to(piece, (tok, LANES)), side)
    for t in range(tok):
        side = jnp.where((sub == pieces) & (lane == t), route_ref[t].astype(F32), side)
    side = side.astype(BF)
    for k in range(out_ref.shape[0]):
        out_ref[k, :, :width] = patches_ref[...]
        out_ref[k, :, width : 2 * width] = tgrad_ref[...]
        out_ref[k, :, 2 * width :] = side


def grads_kernel(y_ref, rows_ref, got_ref, w_ref, turned_ref, grads_ref, onehot_ref, count_ref, back_ref):
    tokens = got_ref.shape[0]
    for k in range(4):
        start = pl.multiple_of(((y_ref[0] + k) % 4) * 128, 128)
        turned_ref[k * 128 : (k + 1) * 128, :] = rows_ref[pl.ds(start, 128), :]
    width = w_ref.shape[1]
    side = got_ref[:, width:]
    sub = lax.broadcasted_iota(jnp.int32, (tokens, LANES), 0) % 8
    lane = lax.broadcasted_iota(jnp.int32, (tokens, LANES), 1)
    group = (
        lax.broadcasted_iota(jnp.int32, (tokens, 64), 0) // 8 == lax.broadcasted_iota(jnp.int32, (tokens, 64), 1)
    )
    group = group.astype(F32).astype(BF)
    down_rows = (((0,), (0,)), ((), ()))
    wide = jnp.where(sub == width // LANES, side.astype(F32), 0.0).astype(BF)
    routes = lax.dot_general(group, wide, down_rows, preferred_element_type=F32).astype(BF)
    routes = jnp.dot(group, routes, preferred_element_type=F32)
    route = jnp.sum(jnp.where(lane == sub, routes, 0.0), axis=1, keepdims=True).astype(jnp.int32)
    dp_of = (lax.broadcasted_iota(jnp.int32, (tokens, 1), 0) // 8) % 8
    image = ((route % 2) * 4 + route // 2) * 8 + dp_of
    onehot = (image == lax.broadcasted_iota(jnp.int32, (tokens, 64), 1)).astype(F32).astype(BF)
    ones = jnp.ones((tokens, LANES), BF)
    count = jnp.maximum(lax.dot_general(onehot, ones, down_rows, preferred_element_type=F32)[:, :1], 1.0)
    onehot_ref[...] = onehot
    count_ref[...] = count
    for j in range(width // LANES):
        piece = jnp.where(sub == j, side.astype(F32), 0.0).astype(BF)
        pool = lax.dot_general(group, piece, down_rows, preferred_element_type=F32)
        image_grad = (pool / count).astype(BF)
        returned = jnp.dot(onehot, image_grad, preferred_element_type=F32)
        cols = slice(j * LANES, (j + 1) * LANES)
        grads_ref[:, cols] = (got_ref[:, cols].astype(F32) + returned).astype(BF)
    back_ref[...] = lax.dot_general(
        grads_ref[...], w_ref[...], (((1,), (1,)), ((), ())), preferred_element_type=F32
    ).astype(BF)


def down_kernel(core_ref, mix_ref, w_ref, onehot_ref, count_ref, own_ref, sent_ref, back_ref, back_bf_ref):
    hid, width = w_ref.shape
    core = core_ref[0]
    back = mix_ref[0, :, hid:].astype(F32)
    for k in range(1, mix_ref.shape[0]):
        back = back + mix_ref[k, :, hid:].astype(F32)
    back_ref[...] = back
    back_bf_ref[...] = back.astype(BF)
    parts = []
    total = None
    for which in (core, 1 - core):
        rows = mix_ref[pl.ds(2 * which, 2), :, :hid].reshape(256, hid)
        part = jnp.dot(rows, w_ref[...], preferred_element_type=F32).astype(BF)
        marks = onehot_ref[pl.ds(pl.multiple_of(which * 256, 256), 256), :]
        image = lax.dot_general(marks, part, (((0,), (0,)), ((), ())), preferred_element_type=F32)
        total = image if total is None else total + image
        parts.append(part)
    mean = (total / count_ref[...]).astype(BF)
    row = lax.broadcasted_iota(jnp.int32, (256, 64), 0)
    image_of = lax.broadcasted_iota(jnp.int32, (256, 64), 1)
    sub = lax.broadcasted_iota(jnp.int32, (256, LANES), 0) % 8
    for which, part, ref in ((core, parts[0], own_ref), (1 - core, parts[1], sent_ref)):
        pick = ((row // 8 + which * 32) == image_of).astype(F32).astype(BF)
        wide = jnp.dot(pick, mean, preferred_element_type=F32)
        packed = jnp.zeros((256, LANES), F32)
        for j in range(width // LANES):
            packed = jnp.where(sub == j, wide[:, j * LANES : (j + 1) * LANES], packed)
        ref[:, :width] = part
        ref[:, width:] = packed.astype(BF)


def local(patches, w_up, w_down, owner_route, tok_grad, pool_grad):
    tok, width = patches.shape
    hid = w_up.shape[1]
    pieces = width // LANES

    got = pl.pallas_call(
        pack_kernel,
        out_shape=jax.ShapeDtypeStruct((8, tok, 2 * width + LANES), BF),
        in_specs=[pl.BlockSpec(memory_space=pltpu.SMEM)] + [pl.BlockSpec(memory_space=pltpu.VMEM)] * 3,
        cost_estimate=pl.CostEstimate(flops=100_000, bytes_accessed=300_000, transcendentals=0),
    )(owner_route, patches, tok_grad, pool_grad)
    got = exchange(got, "dp")
    got = got.reshape(64, 2 * width + LANES)
    got = gather(got, "row", X_GROUPS)
    rows = gather(got[:, :width], "row", CORE_GROUPS)

    up = jnp.dot(rows, w_up, preferred_element_type=F32) * UP_SCALE
    up = up.astype(F16)
    up = exchange(up.reshape(4, 128, hid), "col", Y_GROUPS)
    up = jnp.sum(up.astype(F32), axis=0).astype(F16)
    other = lax.ppermute(up, "col", Z_SWAP)
    own_g, _ = lax.optimization_barrier((got[:, width:], up))

    got_g = gather(own_g, "row", CORE_GROUPS)
    y = lax.axis_index("col") % 4
    turned, grads, onehot, count, back = pl.pallas_call(
        grads_kernel,
        out_shape=[
            jax.ShapeDtypeStruct((512, width), BF),
            jax.ShapeDtypeStruct((512, width), BF),
            jax.ShapeDtypeStruct((512, 64), BF),
            jax.ShapeDtypeStruct((64, 1), F32),
            jax.ShapeDtypeStruct((512, hid), BF),
        ],
        in_specs=[pl.BlockSpec(memory_space=pltpu.SMEM)] + [pl.BlockSpec(memory_space=pltpu.VMEM)] * 3,
        compiler_params=pltpu.CompilerParams(vmem_limit_bytes=24 * 1024 * 1024),
        cost_estimate=pl.CostEstimate(flops=1_000_000, bytes_accessed=100_000, transcendentals=0),
    )(y.astype(jnp.int32).reshape(1), rows, got_g, w_down)

    v = (up.astype(F32) + other.astype(F32)) * (1.0 / UP_SCALE)
    s = jnp.tanh(GELU_SCALE * (v + 0.044715 * v * v * v))
    hidden = (0.5 * v * (1.0 + s)).astype(BF)
    slope = 0.5 * (1.0 + s) + 0.5 * v * (1.0 - s * s) * GELU_SCALE * (1.0 + 3.0 * 0.044715 * v * v)

    mix = jnp.concatenate(
        [jnp.broadcast_to(hidden[None], (4, 128, hid)), back.reshape(4, 128, hid)], axis=2
    )
    mix = exchange(mix, "col", Y_GROUPS)
    hidden = mix[:, :, :hid].reshape(512, hid)
    core = lax.axis_index("row") % 2
    wide = width + LANES
    own, sent, back, back_bf = pl.pallas_call(
        down_kernel,
        out_shape=[jax.ShapeDtypeStruct((256, wide), BF)] * 2
        + [jax.ShapeDtypeStruct((128, hid), F32), jax.ShapeDtypeStruct((128, hid), BF)],
        in_specs=[pl.BlockSpec(memory_space=pltpu.SMEM)] + [pl.BlockSpec(memory_space=pltpu.VMEM)] * 4,
        compiler_params=pltpu.CompilerParams(vmem_limit_bytes=24 * 1024 * 1024),
        cost_estimate=pl.CostEstimate(flops=400_000_000, bytes_accessed=3_000_000, transcendentals=0),
    )(core.astype(jnp.int32).reshape(1), mix, w_down, onehot, count)
    sent = gather(sent, "row", CORE_GROUPS).reshape(2, 256, wide)
    half = own.astype(F32) + lax.dynamic_index_in_dim(sent, 1 - core, 0, keepdims=False).astype(F32)
    half = half.astype(BF).reshape(4, 64, wide)
    back_bf, _ = lax.optimization_barrier((back_bf, half))
    half = exchange(half, "row", X_GROUPS)
    half = jnp.sum(half.astype(F32), axis=0).astype(BF).reshape(8, tok, width + LANES)

    back_other = lax.ppermute(back_bf, "col", Z_SWAP)
    gp = ((back + back_other.astype(F32)) * slope).astype(BF)
    grad_down = lax.dot_general(hidden, grads, (((0,), (0,)), ((), ())), preferred_element_type=F32)
    half, grad_down = lax.optimization_barrier((half, grad_down))
    last = exchange(half, "dp")
    last = jnp.sum(last.astype(F32), axis=0)
    mixed = last[:, :width].astype(BF)
    pooled = last[:pieces, width:].reshape(1, width)

    gps = [gp] + [
        lax.ppermute(gp, "col", [(i, i // 4 * 4 + (i - k) % 4) for i in range(8)]) for k in (1, 2, 3)
    ]
    grad_up = lax.dot_general(
        turned, jnp.concatenate(gps, axis=0), (((0,), (0,)), ((), ())), preferred_element_type=F32
    )
    return (mixed, pooled, grad_up, grad_down)


def solution(mesh):
    in_specs = (
        P(("dp", "row"), "col"),
        P("col", ("dp", "row")),
        P(("dp", "row"), "col"),
        P(("dp", "row")),
        P(("dp", "row"), "col"),
        P(("dp", "row"), "col"),
    )
    out_specs = (
        P(("dp", "row"), "col"),
        P(("dp", "row"), "col"),
        P("col", ("dp", "row")),
        P(("dp", "row"), "col"),
    )
    return jax.shard_map(local, mesh=mesh, in_specs=in_specs, out_specs=out_specs, check_vma=False)
```
